32 devices in a mesh: layer: 4 (over y, x), row: 2 (over core), col: 4 (over z).
Axes of the slice: x: 2, y: 2, z: 4, core: 2. Of those that a mesh axis runs over, the one named last changes fastest.
Arguments:
- density: bfloat16 [2048, 2048], P('row', 'col'), may hold values from -0.25 to 0.25
- hamiltonian: bfloat16 [2048, 2048], P('row', 'col'), may hold values from -6 to 6
- density_mask: int32 [32, 32], P('row', 'col'), may hold values from 0 to 1, as said below
- hamilton_mask: int32 [32, 32], P('row', 'col'), may hold values from 0 to 1, as said below
- filter_mask: int32 [32, 32], P('row', 'col'), may hold values from 0 to 1, as said below
Outputs:
- weighted: bfloat16 [2048, 2048], P('row', 'col')
The draws below stay inside these ranges and needn't reach their ends.
Inputs may be any that keep to these rules, and one draw needn't show every extreme that they name: `density_mask`: each entry is 0 or 1; diagonal blocks are 1. `hamilton_mask`: each entry is 0 or 1; diagonal blocks are 1. `filter_mask`: each entry is 0 or 1; diagonal blocks are 1.
All inputs are finite; a program needn't handle non-finite values.
Results may differ from the reference program's by a relative error of at most 0.005.
Values may be sent and summed in bfloat16 or wider, within the bound.
A program may use at most 64 MiB of HBM per device.

```python
import jax
import jax.numpy as jnp

BS = 64
NB = 32
N = 2048


def block_pattern(key, keep):
    rows = jnp.arange(NB, dtype=jnp.int32)[:, None]
    cols = jnp.arange(NB, dtype=jnp.int32)[None, :]
    coins = jax.random.randint(key, (NB, NB), 0, 8)
    kept = (coins < keep) | (rows == cols)
    return kept.astype(jnp.int32)


def draw_density_mask(key, part):
    return block_pattern(jax.random.fold_in(key, 11), 5)


def draw_hamilton_mask(key, part):
    return block_pattern(jax.random.fold_in(key, 23), 5)


def draw_filter_mask(key, part):
    return block_pattern(jax.random.fold_in(key, 37), 6)


def block_scale(key, dims, split, low, high):
    def one(dim, blocks):
        heights = jax.random.uniform(jax.random.fold_in(jax.random.fold_in(key, 6), dim), (blocks,), jnp.float32, low / len(split), high / len(split))
        return jnp.repeat(jnp.exp(heights), dims[dim] // blocks).reshape((-1,) + (1,) * (len(dims) - dim - 1))

    factor_of = one(*split[0])
    for cut in split[1:]:
        factor_of = factor_of * one(*cut)
    return factor_of


def bell_draw(key, shape, scale, bound, cuts=(), kind=jnp.bfloat16):
    entries = jax.random.normal(key, shape, jnp.float32) * scale
    if len(cuts) > 0:
        entries = block_scale(key, shape, cuts, -0.22, 0.18) * entries
    return jnp.clip(entries, min=-bound, max=bound).astype(kind)


def setup_inputs(seed: int = 0) -> dict:
    key_of = jax.random.split(jax.random.key(seed), 6)
    return {
        "density": bell_draw(key_of[0], (N, N), (N // 4) ** -0.5, 0.25, ((0, 2), (1, 4))),
        "hamiltonian": bell_draw(key_of[1], (N, N), 1.0, 6.0, ((0, 2), (1, 4))),
        "density_mask": draw_density_mask(jax.random.fold_in(key_of[5], 71), 0),
        "hamilton_mask": draw_hamilton_mask(jax.random.fold_in(key_of[5], 71), 0),
        "filter_mask": draw_filter_mask(jax.random.fold_in(key_of[5], 71), 0),
    }


def expand_mask(mask_blocks):
    return jnp.repeat(jnp.repeat(mask_blocks, BS, axis=0), BS, axis=1).astype(jnp.bfloat16)


def reference(density, hamiltonian, density_mask, hamilton_mask, filter_mask):
    masked_p = density * expand_mask(density_mask)
    masked_h = hamiltonian * expand_mask(hamilton_mask)
    product = jnp.dot(masked_p, masked_h, preferred_element_type=jnp.float32).astype(jnp.bfloat16)
    product = product * expand_mask(filter_mask)
    weighted = jnp.dot(product, masked_p, preferred_element_type=jnp.float32)
    return weighted.astype(jnp.bfloat16)
```

```python
import functools

import jax
import jax.numpy as jnp
from jax import lax
from jax.experimental import pallas as pl
from jax.experimental.pallas import tpu as pltpu
from jax.sharding import PartitionSpec as P

BS = 64
BF = jnp.bfloat16
F32 = jnp.float32


def kernel(L, R, Z, nc, p_hbm, h_hbm, pm_ref, hm_ref, fm_ref, out_ref,
           p_in, h_in, em, pg, qg, hg, pc, in_sem, zs, zr, hs, hr, cs, cr_sem, ws, wr):
    l, r, c = lax.axis_index("layer"), lax.axis_index("row"), lax.axis_index("col")
    tr, tc = p_in.shape
    lr = tr // L
    ch = lr // nc
    G = tr // tc
    nb, lb = tr // BS, lr // BS
    lrow = pl.multiple_of(l * lr, lr)

    first = pltpu.make_async_copy(
        p_hbm.at[pl.ds(lrow, lr)], pg.at[c], in_sem.at[0])
    whole_p = pltpu.make_async_copy(p_hbm, p_in, in_sem.at[1])
    whole_h = pltpu.make_async_copy(h_hbm, h_in, in_sem.at[2])
    first.start()
    whole_h.start()
    whole_p.start()

    barrier = pltpu.get_barrier_semaphore()

    def greet(dev):
        pl.semaphore_signal(barrier, inc=1, device_id=dev)

    @pl.when(c > 0)
    def _():
        greet({"col": c - 1})

    @pl.when(c < Z - 1)
    def _():
        greet({"col": c + 1})

    for j in range(1, R):
        greet({"row": lax.rem(r + j, R)})
    for j in range(1, L):
        greet({"layer": lax.rem(l + j, L)})

    spread = (lax.broadcasted_iota(jnp.int32, (tc // BS, tc), 1) // BS
              == lax.broadcasted_iota(jnp.int32, (tc // BS, tc), 0))
    spread = spread.astype(F32).astype(BF)
    for i, m in enumerate((pm_ref, hm_ref, fm_ref)):
        em[i] = jnp.dot(m[...].astype(F32).astype(BF), spread, preferred_element_type=F32)

    def z_copy(buf, ph, k, side, origin, hop):
        view = buf.at[origin, pl.ds(k * ch, ch)]
        to = c + 1 if side == 0 else c - 1
        return pltpu.make_async_remote_copy(
            view, view, zs.at[ph, side, k, hop], zr.at[ph, side, k, hop],
            device_id={"col": to})

    def z_origin(side, d):
        return c - d if side == 0 else c + d

    def z_sends(side, d):
        there = c < Z - 1 if side == 0 else c > 0
        if d == 0:
            return there
        return there & (c >= d if side == 0 else c + d < Z)

    def z_send(buf, ph, k, d):
        for side in range(2):
            @pl.when(z_sends(side, d))
            def _():
                z_copy(buf, ph, k, side, z_origin(side, d), d).start()

    def z_step(buf, ph, k, d):
        for side in range(2):
            @pl.when(c >= d if side == 0 else c + d < Z)
            def _():
                z_copy(buf, ph, k, side, z_origin(side, d), d - 1).wait_recv()
        if d < Z - 1:
            z_send(buf, ph, k, d)

    def z_drain(buf, ph, k):
        for d in range(Z - 1):
            for side in range(2):
                @pl.when(z_sends(side, d))
                def _():
                    z_copy(buf, ph, k, side, z_origin(side, d), d).wait_send()

    def mask_chunk(k):
        for i in range(ch // BS):
            at = k * (ch // BS) + i
            keep = em[0, pl.ds(l * lb + at, 1), :].astype(BF)
            rows = pl.ds(at * BS, BS)
            pg[c, rows, :] = pg[c, rows, :] * keep

    first.wait()
    mask_chunk(0)
    near = jnp.where(c > 0, 1, 0) + jnp.where(c < Z - 1, 1, 0)
    pl.semaphore_wait(barrier, near + (R - 1) + (L - 1))
    z_send(pg, 0, 0, 0)

    def fill(src, dst, e):
        per = tc // BS

        def body(i, carry):
            keep = em[e, pl.ds(i, 1), :].astype(BF)
            dst[r * G + i // per, pl.ds(pl.multiple_of((i % per) * BS, BS), BS), :] = (
                src[pl.ds(pl.multiple_of(i * BS, BS), BS), :] * keep)
            return carry

        lax.fori_loop(0, nb, body, 0)

    def row_copy(buf, ss, rs, j, owner):
        view = buf.at[pl.ds(owner * G, G)]
        return pltpu.make_async_remote_copy(
            view, view, ss.at[j - 1], rs.at[j - 1], device_id={"row": lax.rem(r + j, R)})

    whole_h.wait()
    fill(h_in, hg, 1)
    for j in range(1, R):
        row_copy(hg, hs, hr, j, r).start()
    for k in range(1, nc):
        mask_chunk(k)
        if k == 1:
            z_send(pg, 0, 1, 0)
    whole_p.wait()
    fill(p_in, pc, 0)
    for j in range(1, R):
        row_copy(pc, cs, cr_sem, j, r).start()

    def product(left, right, k):
        def body(o, acc):
            return acc + jnp.dot(left[o, pl.ds(k * ch, ch), :], right[o],
                                 preferred_element_type=F32)

        return lax.fori_loop(0, Z, body, jnp.zeros((ch, tc), F32), unroll=Z if Z <= 4 else 1)

    def w_copy(k, j, owner):
        view = out_ref.at[pl.ds(pl.multiple_of(owner * lr + k * ch, ch), ch)]
        return pltpu.make_async_remote_copy(
            view, view, ws.at[j - 1, k], wr.at[j - 1, k],
            device_id={"layer": lax.rem(l + j, L)})

    for k in range(nc + 1):
        if 1 <= k < nc - 1:
            z_send(pg, 0, k + 1, 0)
        for d in range(1, Z):
            if k < nc:
                z_step(pg, 0, k, d)
            if k > 0:
                z_step(qg, 1, k - 1, d)
        if k < nc:
            if k == 0:
                for j in range(1, R):
                    row_copy(hg, hs, hr, j, lax.rem(r + R - j, R)).wait_recv()
            total = product(pg, hg, k)
            for i in range(ch // BS):
                at = k * (ch // BS) + i
                keep = em[2, pl.ds(l * lb + at, 1), :].astype(BF)
                qg[c, pl.ds(at * BS, BS), :] = total[i * BS:(i + 1) * BS].astype(BF) * keep
            z_send(qg, 1, k, 0)
        if k > 0:
            if k == 1:
                for j in range(1, R):
                    row_copy(pc, cs, cr_sem, j, lax.rem(r + R - j, R)).wait_recv()
            out_ref[pl.ds(pl.multiple_of(l * lr + (k - 1) * ch, ch), ch), :] = (
                product(qg, pc, k - 1).astype(BF))
            for j in range(1, L):
                w_copy(k - 1, j, l).start()

    for k in range(nc):
        z_drain(pg, 0, k)
        z_drain(qg, 1, k)
    for j in range(1, R):
        row_copy(hg, hs, hr, j, r).wait_send()
        row_copy(pc, cs, cr_sem, j, r).wait_send()
    for k in range(nc):
        for j in range(1, L):
            w_copy(k, j, l).wait_send()
            w_copy(k, j, lax.rem(l + L - j, L)).wait_recv()


def solution(mesh):
    L, R, Z = mesh.shape["layer"], mesh.shape["row"], mesh.shape["col"]
    nc = 4 if Z <= 4 else 2

    def local(density, hamiltonian, density_mask, hamilton_mask, filter_mask):
        tr, tc = density.shape
        lr = tr // L
        vmem = pl.BlockSpec(memory_space=pltpu.VMEM)
        hbm = pl.BlockSpec(memory_space=pl.ANY)
        dma = pltpu.SemaphoreType.DMA
        return pl.pallas_call(
            functools.partial(kernel, L, R, Z, nc),
            out_shape=jax.ShapeDtypeStruct((tr, tc), BF),
            in_specs=[hbm, hbm, vmem, vmem, vmem],
            out_specs=vmem,
            scratch_shapes=[
                pltpu.VMEM((tr, tc), BF),
                pltpu.VMEM((tr, tc), BF),
                pltpu.VMEM((3, tr // BS, tc), F32),
                pltpu.VMEM((Z, lr, tc), BF),
                pltpu.VMEM((Z, lr, tc), BF),
                pltpu.VMEM((R * tr // tc, tc, tc), BF),
                pltpu.VMEM((R * tr // tc, tc, tc), BF),
                dma((3,)),
                dma((2, 2, nc, Z - 1)),
                dma((2, 2, nc, Z - 1)),
                dma((R - 1,)),
                dma((R - 1,)),
                dma((R - 1,)),
                dma((R - 1,)),
                dma((L - 1, nc)),
                dma((L - 1, nc)),
            ],
            compiler_params=pltpu.CompilerParams(
                collective_id=0, has_side_effects=True, vmem_limit_bytes=52 * 2**20),
            cost_estimate=pl.CostEstimate(
                flops=4 * lr * tc * tc * Z, bytes_accessed=6 * tr * tc, transcendentals=0),
        )(density, hamiltonian, density_mask, hamilton_mask, filter_mask)

    placed = (P("row", "col"),) * 5
    return jax.shard_map(
        local, mesh=mesh, in_specs=placed, out_specs=P("row", "col"), check_vma=False)
```

```python
import functools

import jax
import jax.numpy as jnp
from jax import lax
from jax.experimental import pallas as pl
from jax.experimental.pallas import tpu as pltpu
from jax.sharding import PartitionSpec as P

BS = 64
BF = jnp.bfloat16
F32 = jnp.float32


def kernel(L, R, Z, nc, p_hbm, h_hbm, pm_hbm, hm_hbm, fm_hbm, out_ref,
           p_in, h_in, m_in, em, acc, pg, qg, hg, pc, in_sem, zs, zr, hs, hr, cs, cr_sem, ws, wr):
    l, r, c = lax.axis_index("layer"), lax.axis_index("row"), lax.axis_index("col")
    tr, tc = p_in.shape
    lr = tr // L
    ch = lr // nc
    G = tr // tc
    nb, lb = tr // BS, lr // BS
    lrow = pl.multiple_of(l * lr, lr)

    first = pltpu.make_async_copy(
        p_hbm.at[pl.ds(lrow, lr)], pg.at[c], in_sem.at[0])
    whole_p = pltpu.make_async_copy(p_hbm, p_in, in_sem.at[1])
    whole_h = pltpu.make_async_copy(h_hbm, h_in, in_sem.at[2])
    masks = [pltpu.make_async_copy(m, m_in.at[i], in_sem.at[3 + i])
             for i, m in enumerate((pm_hbm, hm_hbm, fm_hbm))]
    for m in masks:
        m.start()
    first.start()
    whole_h.start()
    whole_p.start()

    barrier = pltpu.get_barrier_semaphore()

    def greet(dev):
        pl.semaphore_signal(barrier, inc=1, device_id=dev)

    @pl.when(c > 0)
    def _():
        greet({"col": c - 1})

    @pl.when(c < Z - 1)
    def _():
        greet({"col": c + 1})

    for j in range(1, R):
        greet({"row": lax.rem(r + j, R)})
    for j in range(1, L):
        greet({"layer": lax.rem(l + j, L)})

    spread = (lax.broadcasted_iota(jnp.int32, (tc // BS, tc), 1) // BS
              == lax.broadcasted_iota(jnp.int32, (tc // BS, tc), 0))
    spread = spread.astype(F32).astype(BF)
    for i in range(3):
        masks[i].wait()
        em[i] = lax.dot_general(
            m_in[i].astype(F32).astype(BF), spread, (((0,), (0,)), ((), ())),
            preferred_element_type=F32)

    def z_copy(buf, ph, k, side, origin, hop):
        view = buf.at[origin, pl.ds(k * ch, ch)]
        to = c + 1 if side == 0 else c - 1
        return pltpu.make_async_remote_copy(
            view, view, zs.at[ph, side, k, hop], zr.at[ph, side, k, hop],
            device_id={"col": to})

    def z_origin(side, d):
        return c - d if side == 0 else c + d

    def z_sends(side, d):
        there = c < Z - 1 if side == 0 else c > 0
        if d == 0:
            return there
        return there & (c >= d if side == 0 else c + d < Z)

    def z_send(buf, ph, k, d):
        for side in range(2):
            @pl.when(z_sends(side, d))
            def _():
                z_copy(buf, ph, k, side, z_origin(side, d), d).start()

    def z_step(buf, ph, k, d):
        for side in range(2):
            @pl.when(c >= d if side == 0 else c + d < Z)
            def _():
                z_copy(buf, ph, k, side, z_origin(side, d), d - 1).wait_recv()
        if d < Z - 1:
            z_send(buf, ph, k, d)

    def z_drain(buf, ph, k):
        for d in range(Z - 1):
            for side in range(2):
                @pl.when(z_sends(side, d))
                def _():
                    z_copy(buf, ph, k, side, z_origin(side, d), d).wait_send()

    def mask_chunk(k):
        for i in range(ch // BS):
            at = k * (ch // BS) + i
            keep = em[0, pl.ds(l * lb + at, 1), :].astype(BF)
            rows = pl.ds(at * BS, BS)
            pg[c, rows, :] = pg[c, rows, :] * keep

    first.wait()
    near = jnp.where(c > 0, 1, 0) + jnp.where(c < Z - 1, 1, 0)
    for k in range(nc):
        mask_chunk(k)
        if k == 0:
            pl.semaphore_wait(barrier, near + (R - 1) + (L - 1))
        z_send(pg, 0, k, 0)

    def fill(src, dst, e):
        per = tc // BS

        def body(i, carry):
            keep = em[e, pl.ds(i, 1), :].astype(BF)
            dst[r * G + i // per, pl.ds(pl.multiple_of((i % per) * BS, BS), BS), :] = (
                src[pl.ds(pl.multiple_of(i * BS, BS), BS), :] * keep)
            return carry

        lax.fori_loop(0, nb, body, 0)

    def row_copy(buf, ss, rs, j, owner):
        view = buf.at[pl.ds(owner * G, G)]
        return pltpu.make_async_remote_copy(
            view, view, ss.at[j - 1], rs.at[j - 1], device_id={"row": lax.rem(r + j, R)})

    whole_h.wait()
    fill(h_in, hg, 1)
    for j in range(1, R):
        row_copy(hg, hs, hr, j, r).start()
    whole_p.wait()
    fill(p_in, pc, 0)
    for j in range(1, R):
        row_copy(pc, cs, cr_sem, j, r).start()

    def begin(left, right, rows):
        acc[rows, :] = jnp.dot(left[c, rows, :], right[c], preferred_element_type=F32)

    def add(left, right, rows, d):
        for side in range(2):
            @pl.when(c >= d if side == 0 else c + d < Z)
            def _():
                o = z_origin(side, d)
                acc[rows, :] += jnp.dot(left[o, rows, :], right[o], preferred_element_type=F32)

    def w_copy(k, j, owner):
        view = out_ref.at[pl.ds(pl.multiple_of(owner * lr + k * ch, ch), ch)]
        return pltpu.make_async_remote_copy(
            view, view, ws.at[j - 1, k], wr.at[j - 1, k],
            device_id={"layer": lax.rem(l + j, L)})

    everything = pl.ds(0, lr)
    for d in range(1, Z - 1):
        for k in range(nc):
            z_step(pg, 0, k, d)
        if d == 1:
            for j in range(1, R):
                row_copy(hg, hs, hr, j, lax.rem(r + R - j, R)).wait_recv()
            begin(pg, hg, everything)
        add(pg, hg, everything, d)
    for k in range(nc):
        z_step(pg, 0, k, Z - 1)
        add(pg, hg, pl.ds(k * ch, ch), Z - 1)
        for i in range(ch // BS):
            at = k * (ch // BS) + i
            rows = pl.ds(at * BS, BS)
            keep = em[2, pl.ds(l * lb + at, 1), :].astype(BF)
            qg[c, rows, :] = acc[rows, :].astype(BF) * keep
        z_send(qg, 1, k, 0)

    for j in range(1, R):
        row_copy(pc, cs, cr_sem, j, lax.rem(r + R - j, R)).wait_recv()
    for k in range(nc):
        rows = pl.ds(k * ch, ch)
        begin(qg, pc, rows)
        for d in range(1, Z):
            z_step(qg, 1, k, d)
            add(qg, pc, rows, d)
        out_ref[pl.ds(pl.multiple_of(l * lr + k * ch, ch), ch), :] = acc[rows, :].astype(BF)
        for j in range(1, L):
            w_copy(k, j, l).start()

    for k in range(nc):
        z_drain(pg, 0, k)
        z_drain(qg, 1, k)
    for j in range(1, R):
        row_copy(hg, hs, hr, j, r).wait_send()
        row_copy(pc, cs, cr_sem, j, r).wait_send()
    for k in range(nc):
        for j in range(1, L):
            w_copy(k, j, l).wait_send()
            w_copy(k, j, lax.rem(l + L - j, L)).wait_recv()


def solution(mesh):
    L, R, Z = mesh.shape["layer"], mesh.shape["row"], mesh.shape["col"]
    nc = 4 if Z <= 4 else 2

    def local(density, hamiltonian, density_mask, hamilton_mask, filter_mask):
        tr, tc = density.shape
        lr = tr // L
        vmem = pl.BlockSpec(memory_space=pltpu.VMEM)
        hbm = pl.BlockSpec(memory_space=pl.ANY)
        dma = pltpu.SemaphoreType.DMA
        return pl.pallas_call(
            functools.partial(kernel, L, R, Z, nc),
            out_shape=jax.ShapeDtypeStruct((tr, tc), BF),
            in_specs=[hbm] * 5,
            out_specs=vmem,
            scratch_shapes=[
                pltpu.VMEM((tr, tc), BF),
                pltpu.VMEM((tr, tc), BF),
                pltpu.VMEM((3, tc // BS, tr // BS), jnp.int32),
                pltpu.VMEM((3, tr // BS, tc), F32),
                pltpu.VMEM((lr, tc), F32),
                pltpu.VMEM((Z, lr, tc), BF),
                pltpu.VMEM((Z, lr, tc), BF),
                pltpu.VMEM((R * tr // tc, tc, tc), BF),
                pltpu.VMEM((R * tr // tc, tc, tc), BF),
                dma((6,)),
                dma((2, 2, nc, Z - 1)),
                dma((2, 2, nc, Z - 1)),
                dma((R - 1,)),
                dma((R - 1,)),
                dma((R - 1,)),
                dma((R - 1,)),
                dma((L - 1, nc)),
                dma((L - 1, nc)),
            ],
            compiler_params=pltpu.CompilerParams(
                collective_id=0, has_side_effects=True, vmem_limit_bytes=52 * 2**20),
            cost_estimate=pl.CostEstimate(
                flops=4 * lr * tc * tc * Z, bytes_accessed=6 * tr * tc, transcendentals=0),
        )(density, hamiltonian, density_mask.T, hamilton_mask.T, filter_mask.T)

    placed = (P("row", "col"),) * 5
    return jax.shard_map(
        local, mesh=mesh, in_specs=placed, out_specs=P("row", "col"), check_vma=False)
```

```python
import functools

import jax
import jax.numpy as jnp
from jax import lax
from jax.experimental import pallas as pl
from jax.experimental.pallas import tpu as pltpu
from jax.sharding import PartitionSpec as P

BS = 64
BF = jnp.bfloat16
F32 = jnp.float32


def kernel(L, R, Z, nc, p_hbm, h_hbm, pm_hbm, hm_hbm, fm_hbm, out_ref,
           p_in, h_in, m_in, em, acc, pg, qg, hg, pc, in_sem, zs, zr, hs, hr, cs, cr_sem, ws, wr,
           acc_e=None, pe=None, we=None, gs=None, gr=None, fs=None, fr=None, es=None, er=None):
    l, r, c = lax.axis_index("layer"), lax.axis_index("row"), lax.axis_index("col")
    tr, tc = p_in.shape
    lr = tr // L
    ch = lr // nc
    G = tr // tc
    nb, lb = tr // BS, lr // BS
    lrow = pl.multiple_of(l * lr, lr)
    helped = acc_e is not None
    middle = (c > 0) & (c < Z - 1)
    end = jnp.where(c <= 1, 0, Z - 1)

    first = pltpu.make_async_copy(
        p_hbm.at[pl.ds(lrow, lr)], pg.at[c], in_sem.at[0])
    whole_p = pltpu.make_async_copy(p_hbm, p_in, in_sem.at[1])
    whole_h = pltpu.make_async_copy(h_hbm, h_in, in_sem.at[2])
    masks = [pltpu.make_async_copy(m, m_in.at[i], in_sem.at[3 + i])
             for i, m in enumerate((pm_hbm, hm_hbm, fm_hbm))]
    for m in masks:
        m.start()
    first.start()
    whole_h.start()
    whole_p.start()

    barrier = pltpu.get_barrier_semaphore()

    def greet(dev):
        pl.semaphore_signal(barrier, inc=1, device_id=dev)

    @pl.when(c > 0)
    def _():
        greet({"col": c - 1})

    @pl.when(c < Z - 1)
    def _():
        greet({"col": c + 1})

    for j in range(1, R):
        greet({"row": lax.rem(r + j, R)})
    for j in range(1, L):
        greet({"layer": lax.rem(l + j, L)})

    spread = (lax.broadcasted_iota(jnp.int32, (tc // BS, tc), 1) // BS
              == lax.broadcasted_iota(jnp.int32, (tc // BS, tc), 0))
    spread = spread.astype(F32).astype(BF)
    for i in range(3):
        masks[i].wait()
        em[i] = lax.dot_general(
            m_in[i].astype(F32).astype(BF), spread, (((0,), (0,)), ((), ())),
            preferred_element_type=F32)

    def z_copy(buf, ph, k, side, origin, hop):
        view = buf.at[origin, pl.ds(k * ch, ch)]
        to = c + 1 if side == 0 else c - 1
        return pltpu.make_async_remote_copy(
            view, view, zs.at[ph, side, k, hop], zr.at[ph, side, k, hop],
            device_id={"col": to})

    def z_origin(side, d):
        return c - d if side == 0 else c + d

    def z_sends(ph, side, d):
        last = 1 if helped and ph == 1 else 0
        there = c < Z - 1 - last if side == 0 else c > last
        if d == 0:
            return there
        return there & (c >= d if side == 0 else c + d < Z)

    def z_gets(ph, side, d):
        got = c >= d if side == 0 else c + d < Z
        return got & middle if helped and ph == 1 else got

    def z_send(buf, ph, k, d):
        for side in range(2):
            @pl.when(z_sends(ph, side, d))
            def _():
                z_copy(buf, ph, k, side, z_origin(side, d), d).start()

    def z_step(buf, ph, k, d):
        for side in range(2):
            @pl.when(z_gets(ph, side, d))
            def _():
                z_copy(buf, ph, k, side, z_origin(side, d), d - 1).wait_recv()
        if d < Z - 1:
            z_send(buf, ph, k, d)

    def z_drain(buf, ph, k):
        for d in range(Z - 1):
            for side in range(2):
                @pl.when(z_sends(ph, side, d))
                def _():
                    z_copy(buf, ph, k, side, z_origin(side, d), d).wait_send()

    def mask_chunk(k):
        for i in range(ch // BS):
            at = k * (ch // BS) + i
            keep = em[0, pl.ds(l * lb + at, 1), :].astype(BF)
            rows = pl.ds(at * BS, BS)
            pg[c, rows, :] = pg[c, rows, :] * keep

    first.wait()
    near = jnp.where(c > 0, 1, 0) + jnp.where(c < Z - 1, 1, 0)
    for k in range(nc):
        mask_chunk(k)
        if k == 0:
            pl.semaphore_wait(barrier, near + (R - 1) + (L - 1))
        z_send(pg, 0, k, 0)

    def fill(src, dst, e):
        per = tc // BS

        def body(i, carry):
            keep = em[e, pl.ds(i, 1), :].astype(BF)
            dst[r * G + i // per, pl.ds(pl.multiple_of((i % per) * BS, BS), BS), :] = (
                src[pl.ds(pl.multiple_of(i * BS, BS), BS), :] * keep)
            return carry

        lax.fori_loop(0, nb, body, 0)

    def row_copy(buf, ss, rs, j, owner):
        view = buf.at[pl.ds(owner * G, G)]
        return pltpu.make_async_remote_copy(
            view, view, ss.at[j - 1], rs.at[j - 1], device_id={"row": lax.rem(r + j, R)})

    whole_h.wait()
    fill(h_in, hg, 1)
    for j in range(1, R):
        row_copy(hg, hs, hr, j, r).start()
    whole_p.wait()
    fill(p_in, pc, 0)
    for j in range(1, R):
        row_copy(pc, cs, cr_sem, j, r).start()

    def begin(left, right, rows):
        acc[rows, :] = jnp.dot(left[c, rows, :], right[c], preferred_element_type=F32)

    def add(ph, left, right, rows, d):
        for side in range(2):
            @pl.when(z_gets(ph, side, d))
            def _():
                o = z_origin(side, d)
                acc[rows, :] += jnp.dot(left[o, rows, :], right[o], preferred_element_type=F32)
                if helped and ph == 1:
                    acc_e[...] += jnp.dot(left[o, rows, :], pe[o], preferred_element_type=F32)

    def share(row, layer):
        start = layer * lr
        return pe.at[row * G + start // tc, pl.ds(pl.multiple_of(start % tc, lr), lr)]

    def share_copy(j, layer):
        return pltpu.make_async_remote_copy(
            share(r, layer), share(r, layer), gs.at[j - 1], gr.at[j - 1],
            device_id={"layer": lax.rem(l + j, L)})

    def pass_copy(q, i, row, layer):
        return pltpu.make_async_remote_copy(
            share(row, layer), share(row, layer), fs.at[q - 1, i], fr.at[q - 1, i],
            device_id={"row": lax.rem(r + q, R)})

    def end_copy(k):
        return pltpu.make_async_remote_copy(
            we.at[pl.ds(k * ch, ch)],
            out_ref.at[pl.ds(pl.multiple_of(l * lr + k * ch, ch), ch)],
            es.at[k], er.at[k], device_id={"col": jnp.where(c == 1, 0, jnp.where(c == 0, 1, jnp.where(c == Z - 1, Z - 2, Z - 1)))})

    def w_copy(k, j, owner):
        view = out_ref.at[pl.ds(pl.multiple_of(owner * lr + k * ch, ch), ch)]
        return pltpu.make_async_remote_copy(
            view, view, ws.at[j - 1, k], wr.at[j - 1, k],
            device_id={"layer": lax.rem(l + j, L)})

    everything = pl.ds(0, lr)
    for d in range(1, Z - 1):
        for k in range(nc):
            z_step(pg, 0, k, d)
        if d == 1:
            for j in range(1, R):
                row_copy(hg, hs, hr, j, lax.rem(r + R - j, R)).wait_recv()
            begin(pg, hg, everything)
            if helped:
                @pl.when(middle)
                def _():
                    share(r, l)[...] = pg[end]
                    for j in range(1, L):
                        share_copy(j, l).start()
                    for q in range(1, R):
                        pass_copy(q, 0, r, l).start()
        add(0, pg, hg, everything, d)
    for k in range(nc):
        z_step(pg, 0, k, Z - 1)
        add(0, pg, hg, pl.ds(k * ch, ch), Z - 1)
        for i in range(ch // BS):
            at = k * (ch // BS) + i
            rows = pl.ds(at * BS, BS)
            keep = em[2, pl.ds(l * lb + at, 1), :].astype(BF)
            qg[c, rows, :] = acc[rows, :].astype(BF) * keep
        z_send(qg, 1, k, 0)

    for j in range(1, R):
        row_copy(pc, cs, cr_sem, j, lax.rem(r + R - j, R)).wait_recv()

    def w_sends(k):
        for j in range(1, L):
            w_copy(k, j, l).start()

    def last_product(k):
        rows = pl.ds(k * ch, ch)
        begin(qg, pc, rows)
        if helped:
            if k == 0:
                for j in range(1, L):
                    came = lax.rem(l + L - j, L)
                    share_copy(j, came).wait_recv()
                    for q in range(1, R):
                        pass_copy(q, j, r, came).start()
                for q in range(1, R):
                    row = lax.rem(r + R - q, R)
                    for j in range(L):
                        pass_copy(q, j, row, lax.rem(l + L - j, L)).wait_recv()
            acc_e[...] = jnp.dot(qg[c, rows, :], pe[c], preferred_element_type=F32)
        for d in range(1, Z):
            z_step(qg, 1, k, d)
            add(1, qg, pc, rows, d)
        if helped:
            we[rows, :] = acc_e[...].astype(BF)
            end_copy(k).start()
        out_ref[pl.ds(pl.multiple_of(l * lr + k * ch, ch), ch), :] = acc[rows, :].astype(BF)
        w_sends(k)

    if helped:
        @pl.when(middle)
        def _():
            for k in range(nc):
                last_product(k)
            for k in range(nc):
                end_copy(k).wait_send()
            for j in range(1, L):
                share_copy(j, l).wait_send()
            for q in range(1, R):
                for j in range(L):
                    pass_copy(q, j, r, lax.rem(l + L - j, L)).wait_send()

        @pl.when(jnp.logical_not(middle))
        def _():
            for k in range(nc):
                end_copy(k).wait_recv()
                w_sends(k)
    else:
        for k in range(nc):
            last_product(k)

    for k in range(nc):
        z_drain(pg, 0, k)
        z_drain(qg, 1, k)
    for j in range(1, R):
        row_copy(hg, hs, hr, j, r).wait_send()
        row_copy(pc, cs, cr_sem, j, r).wait_send()
    for k in range(nc):
        for j in range(1, L):
            w_copy(k, j, l).wait_send()
            w_copy(k, j, lax.rem(l + L - j, L)).wait_recv()


def solution(mesh):
    L, R, Z = mesh.shape["layer"], mesh.shape["row"], mesh.shape["col"]
    nc = 4 if Z <= 4 else 2

    def local(density, hamiltonian, density_mask, hamilton_mask, filter_mask):
        tr, tc = density.shape
        lr = tr // L
        vmem = pl.BlockSpec(memory_space=pltpu.VMEM)
        hbm = pl.BlockSpec(memory_space=pltpu.HBM)
        dma = pltpu.SemaphoreType.DMA
        extra = [
            pltpu.VMEM((lr // nc, tc), F32),
            pltpu.VMEM((R * tr // tc, tc, tc), BF),
            pltpu.VMEM((lr, tc), BF),
            dma((L - 1,)),
            dma((L - 1,)),
            dma((R - 1, L)),
            dma((R - 1, L)),
            dma((nc,)),
            dma((nc,)),
        ] if Z == 4 else []
        return pl.pallas_call(
            functools.partial(kernel, L, R, Z, nc),
            out_shape=jax.ShapeDtypeStruct((tr, tc), BF),
            in_specs=[hbm] * 5,
            out_specs=vmem,
            scratch_shapes=[
                pltpu.VMEM((tr, tc), BF),
                pltpu.VMEM((tr, tc), BF),
                pltpu.VMEM((3, tc // BS, tr // BS), jnp.int32),
                pltpu.VMEM((3, tr // BS, tc), F32),
                pltpu.VMEM((lr, tc), F32),
                pltpu.VMEM((Z, lr, tc), BF),
                pltpu.VMEM((Z, lr, tc), BF),
                pltpu.VMEM((R * tr // tc, tc, tc), BF),
                pltpu.VMEM((R * tr // tc, tc, tc), BF),
                dma((6,)),
                dma((2, 2, nc, Z - 1)),
                dma((2, 2, nc, Z - 1)),
                dma((R - 1,)),
                dma((R - 1,)),
                dma((R - 1,)),
                dma((R - 1,)),
                dma((L - 1, nc)),
                dma((L - 1, nc)),
            ] + extra,
            compiler_params=pltpu.CompilerParams(
                collective_id=0, has_side_effects=True, vmem_limit_bytes=52 * 2**20),
            cost_estimate=pl.CostEstimate(
                flops=4 * lr * tc * tc * Z, bytes_accessed=6 * tr * tc, transcendentals=0),
        )(density, hamiltonian, density_mask.T, hamilton_mask.T, filter_mask.T)

    placed = (P("row", "col"),) * 5
    return jax.shard_map(
        local, mesh=mesh, in_specs=placed, out_specs=P("row", "col"), check_vma=False)
```

```python
import functools

import jax
import jax.numpy as jnp
from jax import lax
from jax.experimental import pallas as pl
from jax.experimental.pallas import tpu as pltpu
from jax.sharding import PartitionSpec as P

BS = 64
BF = jnp.bfloat16
F32 = jnp.float32


def kernel(L, R, Z, nc, p_hbm, h_hbm, m_in, out_ref,
           p_in, h_in, em, acc, pg, qg, hg, pc, in_sem, zs, zr, hs, hr, cs, cr_sem, ws, wr,
           acc_e=None, pe=None, we=None, gs=None, gr=None, fs=None, fr=None, es=None, er=None,
           xs=None, xr=None):
    l, r, c = lax.axis_index("layer"), lax.axis_index("row"), lax.axis_index("col")
    tr, tc = p_in.shape
    lr = tr // L
    ch = lr // nc
    G = tr // tc
    nb, lb = tr // BS, lr // BS
    lrow = pl.multiple_of(l * lr, lr)
    nw = nc // 2
    cw = lr // nw
    helped = acc_e is not None
    middle = (c > 0) & (c < Z - 1)
    end = jnp.where(c <= 1, 0, Z - 1)

    first = pltpu.make_async_copy(
        p_hbm.at[pl.ds(lrow, lr)], pg.at[c], in_sem.at[0])
    whole_p = pltpu.make_async_copy(p_hbm, p_in, in_sem.at[1])
    whole_h = pltpu.make_async_copy(h_hbm, h_in, in_sem.at[2])
    first.start()
    whole_h.start()
    whole_p.start()

    barrier = pltpu.get_barrier_semaphore()

    def greet(dev):
        pl.semaphore_signal(barrier, inc=1, device_id=dev)

    @pl.when(c > 0)
    def _():
        greet({"col": c - 1})

    @pl.when(c < Z - 1)
    def _():
        greet({"col": c + 1})

    for j in range(1, R):
        greet({"row": lax.rem(r + j, R)})
    for j in range(1, L):
        greet({"layer": lax.rem(l + j, L)})

    spread = (lax.broadcasted_iota(jnp.int32, (tc // BS, tc), 1) // BS
              == lax.broadcasted_iota(jnp.int32, (tc // BS, tc), 0))
    spread = spread.astype(F32).astype(BF)
    for i in range(3):
        em[i] = lax.dot_general(
            m_in[i].astype(F32).astype(BF), spread, (((0,), (0,)), ((), ())),
            preferred_element_type=F32)

    def z_copy(buf, ph, k, side, origin, hop):
        view = buf.at[origin, pl.ds(k * ch, ch)]
        to = c + 1 if side == 0 else c - 1
        return pltpu.make_async_remote_copy(
            view, view, zs.at[ph, side, k, hop], zr.at[ph, side, k, hop],
            device_id={"col": to})

    def z_origin(side, d):
        return c - d if side == 0 else c + d

    def z_sends(ph, side, d):
        last = 1 if helped and ph == 1 else 0
        there = c < Z - 1 - last if side == 0 else c > last
        if d == 0:
            return there
        return there & (c >= d if side == 0 else c + d < Z)

    def z_gets(ph, side, d):
        got = c >= d if side == 0 else c + d < Z
        return got & middle if helped and ph == 1 else got

    def z_send(buf, ph, k, d):
        for side in range(2):
            @pl.when(z_sends(ph, side, d))
            def _():
                z_copy(buf, ph, k, side, z_origin(side, d), d).start()

    def z_step(buf, ph, k, d):
        for side in range(2):
            @pl.when(z_gets(ph, side, d))
            def _():
                z_copy(buf, ph, k, side, z_origin(side, d), d - 1).wait_recv()
        if d < Z - 1:
            z_send(buf, ph, k, d)

    def z_drain(buf, ph, k):
        for d in range(Z - 1):
            for side in range(2):
                @pl.when(z_sends(ph, side, d))
                def _():
                    z_copy(buf, ph, k, side, z_origin(side, d), d).wait_send()

    def mask_chunk(k):
        for i in range(ch // BS):
            at = k * (ch // BS) + i
            keep = em[0, pl.ds(l * lb + at, 1), :].astype(BF)
            rows = pl.ds(at * BS, BS)
            pg[c, rows, :] = pg[c, rows, :] * keep

    first.wait()
    near = jnp.where(c > 0, 1, 0) + jnp.where(c < Z - 1, 1, 0)
    for k in range(nc):
        mask_chunk(k)
        if k == 0:
            pl.semaphore_wait(barrier, near + (R - 1) + (L - 1))
        z_send(pg, 0, k, 0)

    def fill(src, dst, e):
        per = tc // BS

        def body(i, carry):
            keep = em[e, pl.ds(i, 1), :].astype(BF)
            dst[r * G + i // per, pl.ds(pl.multiple_of((i % per) * BS, BS), BS), :] = (
                src[pl.ds(pl.multiple_of(i * BS, BS), BS), :] * keep)
            return carry

        lax.fori_loop(0, nb, body, 0)

    def row_copy(buf, ss, rs, j, owner):
        view = buf.at[pl.ds(owner * G, G)]
        return pltpu.make_async_remote_copy(
            view, view, ss.at[j - 1], rs.at[j - 1], device_id={"row": lax.rem(r + j, R)})

    whole_h.wait()
    fill(h_in, hg, 1)
    for j in range(1, R):
        row_copy(hg, hs, hr, j, r).start()
    whole_p.wait()
    fill(p_in, pc, 0)
    for j in range(1, R):
        row_copy(pc, cs, cr_sem, j, r).start()

    def begin(left, right, rows):
        acc[rows, :] = jnp.dot(left[c, rows, :], right[c], preferred_element_type=F32)

    def add(ph, left, right, rows, d):
        for side in range(2):
            @pl.when(z_gets(ph, side, d))
            def _():
                o = z_origin(side, d)
                acc[rows, :] += jnp.dot(left[o, rows, :], right[o], preferred_element_type=F32)
                if helped and ph == 1:
                    acc_e[...] += jnp.dot(left[o, rows, :], pe[o], preferred_element_type=F32)

    def share(row, layer):
        start = layer * lr
        return pe.at[row * G + start // tc, pl.ds(pl.multiple_of(start % tc, lr), lr)]

    def flip(t):
        return (l, l + 1 - 2 * (l % 2), l + 2 - 4 * (l // 2), L - 1 - l)[t]

    def share_copy(t, layer):
        return pltpu.make_async_remote_copy(
            share(r, layer), share(r, layer), gs.at[t - 1], gr.at[t - 1],
            device_id={"layer": flip(t)})

    beside = jnp.where(c == 1, 0, jnp.where(c == 0, 1, jnp.where(c == Z - 1, Z - 2, Z - 1)))

    def far_copy():
        start = flip(3) * lr
        view = pc.at[r * G + start // tc, pl.ds(pl.multiple_of(start % tc, lr), lr)]
        return pltpu.make_async_remote_copy(
            view, share(r, flip(3)), xs.at[0], xr.at[0], device_id={"col": beside})

    def pass_copy(q, i, row, layer):
        return pltpu.make_async_remote_copy(
            share(row, layer), share(row, layer), fs.at[q - 1, i], fr.at[q - 1, i],
            device_id={"row": lax.rem(r + q, R)})

    def end_copy(k):
        return pltpu.make_async_remote_copy(
            we.at[pl.ds(k * cw, cw)],
            out_ref.at[pl.ds(pl.multiple_of(l * lr + k * cw, cw), cw)],
            es.at[k], er.at[k], device_id={"col": beside})

    def w_copy(k, j, owner):
        view = out_ref.at[pl.ds(pl.multiple_of(owner * lr + k * ch, ch), ch)]
        return pltpu.make_async_remote_copy(
            view, view, ws.at[j - 1, k], wr.at[j - 1, k],
            device_id={"layer": lax.rem(l + j, L)})

    everything = pl.ds(0, lr)
    for d in range(1, Z - 1):
        for k in range(nc):
            z_step(pg, 0, k, d)
        if d == 1:
            for j in range(1, R):
                row_copy(hg, hs, hr, j, lax.rem(r + R - j, R)).wait_recv()
            begin(pg, hg, everything)
            if helped:
                @pl.when(jnp.logical_not(middle))
                def _():
                    far_copy().start()

                @pl.when(middle)
                def _():
                    share(r, l)[...] = pg[end]
                    for t in (1, 2):
                        share_copy(t, l).start()
                    for q in range(1, R):
                        pass_copy(q, 0, r, l).start()
        add(0, pg, hg, everything, d)
    for k in range(nc):
        z_step(pg, 0, k, Z - 1)
        add(0, pg, hg, pl.ds(k * ch, ch), Z - 1)
        for i in range(ch // BS):
            at = k * (ch // BS) + i
            rows = pl.ds(at * BS, BS)
            keep = em[2, pl.ds(l * lb + at, 1), :].astype(BF)
            qg[c, rows, :] = acc[rows, :].astype(BF) * keep
        z_send(qg, 1, k, 0)

    for j in range(1, R):
        row_copy(pc, cs, cr_sem, j, lax.rem(r + R - j, R)).wait_recv()

    def turn_copy(k, t, owner, lane):
        view = out_ref.at[pl.ds(pl.multiple_of(owner * lr + k * ch, ch), ch)]
        return pltpu.make_async_remote_copy(
            view, view, ws.at[lane, k], wr.at[lane, k], device_id={"layer": flip(t)})

    def via(k):
        return 1 + k % 2

    def w_sends(kw):
        if not helped:
            for k in (2 * kw, 2 * kw + 1):
                for j in range(1, L):
                    w_copy(k, j, l).start()
            return
        for i in range(2):
            for t in (1, 2):
                turn_copy(2 * kw + (i + t + 1) % 2, t, l, t - 1).start()
        if kw > 0:
            w_turns(kw - 1)

    def w_turns(kw):
        for k in (2 * kw, 2 * kw + 1):
            t = via(k)
            turn_copy(k, t, flip(t), t - 1).wait_recv()
            turn_copy(k, 3 - t, flip(t), 2).start()

    def last_product(kw):
        rows = pl.ds(kw * cw, cw)
        begin(qg, pc, rows)
        if helped:
            if kw == 0:
                for t in (1, 2):
                    share_copy(t, flip(t)).wait_recv()
                    for q in range(1, R):
                        pass_copy(q, t, r, flip(t)).start()
                far_copy().wait_recv()
                for q in range(1, R):
                    pass_copy(q, 3, r, flip(3)).start()
                for q in range(1, R):
                    row = lax.rem(r + R - q, R)
                    for t in range(L):
                        pass_copy(q, t, row, flip(t)).wait_recv()
            acc_e[...] = jnp.dot(qg[c, rows, :], pe[c], preferred_element_type=F32)
        for d in range(1, Z):
            for k in (2 * kw, 2 * kw + 1):
                z_step(qg, 1, k, d)
            add(1, qg, pc, rows, d)
        if helped:
            we[rows, :] = acc_e[...].astype(BF)
            end_copy(kw).start()
        out_ref[pl.ds(pl.multiple_of(l * lr + kw * cw, cw), cw), :] = acc[rows, :].astype(BF)
        w_sends(kw)

    if helped:
        @pl.when(middle)
        def _():
            for kw in range(nw):
                last_product(kw)

        @pl.when(jnp.logical_not(middle))
        def _():
            for kw in range(nw):
                end_copy(kw).wait_recv()
                w_sends(kw)

        w_turns(nw - 1)

        @pl.when(middle)
        def _():
            for kw in range(nw):
                end_copy(kw).wait_send()
            for t in (1, 2):
                share_copy(t, l).wait_send()
            for q in range(1, R):
                for t in range(L):
                    pass_copy(q, t, r, flip(t)).wait_send()

        @pl.when(jnp.logical_not(middle))
        def _():
            far_copy().wait_send()
    else:
        for kw in range(nw):
            last_product(kw)

    for k in range(nc):
        z_drain(pg, 0, k)
        z_drain(qg, 1, k)
    for j in range(1, R):
        row_copy(hg, hs, hr, j, r).wait_send()
        row_copy(pc, cs, cr_sem, j, r).wait_send()
    for k in range(nc):
        if helped:
            for t in (1, 2):
                turn_copy(k, t, l, t - 1).wait_send()
                if t != via(k):
                    turn_copy(k, t, flip(t), t - 1).wait_recv()
            turn_copy(k, 3 - via(k), flip(via(k)), 2).wait_send()
            turn_copy(k, via(k), flip(3), 2).wait_recv()
            continue
        for j in range(1, L):
            w_copy(k, j, l).wait_send()
            w_copy(k, j, lax.rem(l + L - j, L)).wait_recv()


def solution(mesh):
    L, R, Z = mesh.shape["layer"], mesh.shape["row"], mesh.shape["col"]
    nc = 4 if Z <= 4 else 2

    def local(density, hamiltonian, density_mask, hamilton_mask, filter_mask):
        tr, tc = density.shape
        lr = tr // L
        vmem = pl.BlockSpec(memory_space=pltpu.VMEM)
        hbm = pl.BlockSpec(memory_space=pltpu.HBM)
        dma = pltpu.SemaphoreType.DMA
        extra = [
            pltpu.VMEM((2 * lr // nc, tc), F32),
            pltpu.VMEM((R * tr // tc, tc, tc), BF),
            pltpu.VMEM((lr, tc), BF),
            dma((2,)),
            dma((2,)),
            dma((R - 1, L)),
            dma((R - 1, L)),
            dma((nc // 2,)),
            dma((nc // 2,)),
            dma((1,)),
            dma((1,)),
        ] if Z == 4 and L == 4 else []
        return pl.pallas_call(
            functools.partial(kernel, L, R, Z, nc),
            out_shape=jax.ShapeDtypeStruct((tr, tc), BF),
            in_specs=[hbm, hbm, vmem],
            out_specs=vmem,
            scratch_shapes=[
                pltpu.VMEM((tr, tc), BF),
                pltpu.VMEM((tr, tc), BF),
                pltpu.VMEM((3, tr // BS, tc), F32),
                pltpu.VMEM((lr, tc), F32),
                pltpu.VMEM((Z, lr, tc), BF),
                pltpu.VMEM((Z, lr, tc), BF),
                pltpu.VMEM((R * tr // tc, tc, tc), BF),
                pltpu.VMEM((R * tr // tc, tc, tc), BF),
                dma((3,)),
                dma((2, 2, nc, Z - 1)),
                dma((2, 2, nc, Z - 1)),
                dma((R - 1,)),
                dma((R - 1,)),
                dma((R - 1,)),
                dma((R - 1,)),
                dma((L - 1, nc)),
                dma((L - 1, nc)),
            ] + extra,
            compiler_params=pltpu.CompilerParams(
                collective_id=0, has_side_effects=True, vmem_limit_bytes=52 * 2**20),
            cost_estimate=pl.CostEstimate(
                flops=4 * lr * tc * tc * Z, bytes_accessed=6 * tr * tc, transcendentals=0),
        )(density, hamiltonian, jnp.stack([density_mask.T, hamilton_mask.T, filter_mask.T]))

    placed = (P("row", "col"),) * 5
    return jax.shard_map(
        local, mesh=mesh, in_specs=placed, out_specs=P("row", "col"), check_vma=False)
```

```python
import functools

import jax
import jax.numpy as jnp
from jax import lax
from jax.experimental import pallas as pl
from jax.experimental.pallas import tpu as pltpu
from jax.sharding import PartitionSpec as P

BS = 64
BF = jnp.bfloat16
F32 = jnp.float32


def kernel(L, R, Z, nc, p_hbm, h_hbm, m_in, out_ref,
           p_in, h_in, em, acc, pg, qg, hg, pc, in_sem, zs, zr, hs, hr, cs, cr_sem, ws, wr,
           acc_e=None, pe=None, we=None, gs=None, gr=None, fs=None, fr=None, es=None, er=None,
           xs=None, xr=None):
    l, r, c = lax.axis_index("layer"), lax.axis_index("row"), lax.axis_index("col")
    tr, tc = p_in.shape
    lr = tr // L
    ch = lr // nc
    G = tr // tc
    nb, lb = tr // BS, lr // BS
    lrow = pl.multiple_of(l * lr, lr)
    nw = nc // 2
    cw = lr // nw
    helped = acc_e is not None
    middle = (c > 0) & (c < Z - 1)
    end = jnp.where(c <= 1, 0, Z - 1)

    first = pltpu.make_async_copy(
        p_hbm.at[pl.ds(lrow, lr)], pg.at[c], in_sem.at[0])
    whole_p = pltpu.make_async_copy(p_hbm, p_in, in_sem.at[1])
    whole_h = pltpu.make_async_copy(h_hbm, h_in, in_sem.at[2])
    first.start()
    whole_h.start()
    whole_p.start()

    barrier = pltpu.get_barrier_semaphore()

    def greet(dev):
        pl.semaphore_signal(barrier, inc=1, device_id=dev)

    @pl.when(c > 0)
    def _():
        greet({"col": c - 1})

    @pl.when(c < Z - 1)
    def _():
        greet({"col": c + 1})

    for j in range(1, R):
        greet({"row": lax.rem(r + j, R)})
    for j in range(1, L):
        greet({"layer": lax.rem(l + j, L)})

    spread = (lax.broadcasted_iota(jnp.int32, (tc // BS, tc), 1) // BS
              == lax.broadcasted_iota(jnp.int32, (tc // BS, tc), 0))
    spread = spread.astype(F32).astype(BF)
    for i in range(3):
        em[i] = lax.dot_general(
            m_in[i].astype(F32).astype(BF), spread, (((0,), (0,)), ((), ())),
            preferred_element_type=F32)

    def z_copy(buf, ph, k, side, origin, hop):
        view = buf.at[origin, pl.ds(k * ch, ch)]
        to = c + 1 if side == 0 else c - 1
        return pltpu.make_async_remote_copy(
            view, view, zs.at[ph, side, k, hop], zr.at[ph, side, k, hop],
            device_id={"col": to})

    def z_origin(side, d):
        return c - d if side == 0 else c + d

    def z_sends(ph, side, d):
        last = 1 if helped and ph == 1 else 0
        there = c < Z - 1 - last if side == 0 else c > last
        if d == 0:
            return there
        return there & (c >= d if side == 0 else c + d < Z)

    def z_gets(ph, side, d):
        got = c >= d if side == 0 else c + d < Z
        return got & middle if helped and ph == 1 else got

    def z_send(buf, ph, k, d):
        for side in range(2):
            @pl.when(z_sends(ph, side, d))
            def _():
                z_copy(buf, ph, k, side, z_origin(side, d), d).start()

    def z_step(buf, ph, k, d):
        for side in range(2):
            @pl.when(z_gets(ph, side, d))
            def _():
                z_copy(buf, ph, k, side, z_origin(side, d), d - 1).wait_recv()
        if d < Z - 1:
            z_send(buf, ph, k, d)

    def z_drain(buf, ph, k):
        for d in range(Z - 1):
            for side in range(2):
                @pl.when(z_sends(ph, side, d))
                def _():
                    z_copy(buf, ph, k, side, z_origin(side, d), d).wait_send()

    def mask_chunk(k):
        for i in range(ch // BS):
            at = k * (ch // BS) + i
            keep = em[0, pl.ds(l * lb + at, 1), :].astype(BF)
            rows = pl.ds(at * BS, BS)
            pg[c, rows, :] = pg[c, rows, :] * keep

    first.wait()
    near = jnp.where(c > 0, 1, 0) + jnp.where(c < Z - 1, 1, 0)
    for k in range(nc):
        mask_chunk(k)
        if k == 0:
            pl.semaphore_wait(barrier, near + (R - 1) + (L - 1))
        z_send(pg, 0, k, 0)

    def fill(src, dst, e):
        per = tc // BS

        def body(i, carry):
            keep = em[e, pl.ds(i, 1), :].astype(BF)
            dst[r * G + i // per, pl.ds(pl.multiple_of((i % per) * BS, BS), BS), :] = (
                src[pl.ds(pl.multiple_of(i * BS, BS), BS), :] * keep)
            return carry

        lax.fori_loop(0, nb, body, 0)

    def row_copy(buf, ss, rs, j, owner):
        view = buf.at[pl.ds(owner * G, G)]
        return pltpu.make_async_remote_copy(
            view, view, ss.at[j - 1], rs.at[j - 1], device_id={"row": lax.rem(r + j, R)})

    whole_h.wait()
    fill(h_in, hg, 1)
    for j in range(1, R):
        row_copy(hg, hs, hr, j, r).start()
    whole_p.wait()
    fill(p_in, pc, 0)
    for j in range(1, R):
        row_copy(pc, cs, cr_sem, j, r).start()

    def begin(left, right, rows):
        acc[rows, :] = jnp.dot(left[c, rows, :], right[c], preferred_element_type=F32)

    def add(ph, left, right, rows, d):
        for side in range(2):
            @pl.when(z_gets(ph, side, d))
            def _():
                o = z_origin(side, d)
                if right is pe and helped:
                    acc_e[...] += jnp.dot(left[o, rows, :], pe[o], preferred_element_type=F32)
                else:
                    acc[rows, :] += jnp.dot(left[o, rows, :], right[o], preferred_element_type=F32)

    def share(row, layer):
        start = layer * lr
        return pe.at[row * G + start // tc, pl.ds(pl.multiple_of(start % tc, lr), lr)]

    def flip(t):
        return (l, l + 1 - 2 * (l % 2), l + 2 - 4 * (l // 2), L - 1 - l)[t]

    def share_copy(t, layer):
        return pltpu.make_async_remote_copy(
            share(r, layer), share(r, layer), gs.at[t - 1], gr.at[t - 1],
            device_id={"layer": flip(t)})

    beside = jnp.where(c == 1, 0, jnp.where(c == 0, 1, jnp.where(c == Z - 1, Z - 2, Z - 1)))

    def far_copy():
        start = flip(3) * lr
        view = pc.at[r * G + start // tc, pl.ds(pl.multiple_of(start % tc, lr), lr)]
        return pltpu.make_async_remote_copy(
            view, share(r, flip(3)), xs.at[0], xr.at[0], device_id={"col": beside})

    def pass_copy(q, i, row, layer):
        return pltpu.make_async_remote_copy(
            share(row, layer), share(row, layer), fs.at[q - 1, i], fr.at[q - 1, i],
            device_id={"row": lax.rem(r + q, R)})

    def end_copy(k):
        return pltpu.make_async_remote_copy(
            we.at[pl.ds(k * ch, ch)],
            out_ref.at[pl.ds(pl.multiple_of(l * lr + k * ch, ch), ch)],
            es.at[k], er.at[k], device_id={"col": beside})

    def w_copy(k, j, owner):
        view = out_ref.at[pl.ds(pl.multiple_of(owner * lr + k * ch, ch), ch)]
        return pltpu.make_async_remote_copy(
            view, view, ws.at[j - 1, k], wr.at[j - 1, k],
            device_id={"layer": lax.rem(l + j, L)})

    everything = pl.ds(0, lr)
    for d in range(1, Z - 1):
        for k in range(nc):
            z_step(pg, 0, k, d)
        if d == 1:
            for j in range(1, R):
                row_copy(hg, hs, hr, j, lax.rem(r + R - j, R)).wait_recv()
            begin(pg, hg, everything)
            if helped:
                @pl.when(jnp.logical_not(middle))
                def _():
                    far_copy().start()

                @pl.when(middle)
                def _():
                    share(r, l)[...] = pg[end]
                    for t in (1, 2):
                        share_copy(t, l).start()
                    for q in range(1, R):
                        pass_copy(q, 0, r, l).start()
        add(0, pg, hg, everything, d)
    for k in range(nc):
        z_step(pg, 0, k, Z - 1)
        add(0, pg, hg, pl.ds(k * ch, ch), Z - 1)
        for i in range(ch // BS):
            at = k * (ch // BS) + i
            rows = pl.ds(at * BS, BS)
            keep = em[2, pl.ds(l * lb + at, 1), :].astype(BF)
            qg[c, rows, :] = acc[rows, :].astype(BF) * keep
        z_send(qg, 1, k, 0)

    for j in range(1, R):
        row_copy(pc, cs, cr_sem, j, lax.rem(r + R - j, R)).wait_recv()

    def turn_copy(k, t, owner, lane):
        view = out_ref.at[pl.ds(pl.multiple_of(owner * lr + k * ch, ch), ch)]
        return pltpu.make_async_remote_copy(
            view, view, ws.at[lane, k], wr.at[lane, k], device_id={"layer": flip(t)})

    def via(k):
        return 1 + k % 2

    def w_sends(kw):
        if not helped:
            for k in (2 * kw, 2 * kw + 1):
                for j in range(1, L):
                    w_copy(k, j, l).start()
            return
        for i in range(2):
            for t in (1, 2):
                turn_copy(2 * kw + (i + t + 1) % 2, t, l, t - 1).start()
        if kw > 0:
            w_turn(2 * kw - 2)
            w_turn(2 * kw - 1)

    def w_turn(k):
        t = via(k)
        turn_copy(k, t, flip(t), t - 1).wait_recv()
        turn_copy(k, 3 - t, flip(t), 2).start()

    def last_product(kw):
        rows = pl.ds(kw * cw, cw)
        begin(qg, pc, rows)
        if helped:
            if kw == 0:
                for t in (1, 2):
                    share_copy(t, flip(t)).wait_recv()
                    for q in range(1, R):
                        pass_copy(q, t, r, flip(t)).start()
                far_copy().wait_recv()
                for q in range(1, R):
                    pass_copy(q, 3, r, flip(3)).start()
                for q in range(1, R):
                    row = lax.rem(r + R - q, R)
                    for t in range(L):
                        pass_copy(q, t, row, flip(t)).wait_recv()
            acc_e[...] = jnp.dot(qg[c, rows, :], pe[c], preferred_element_type=F32)
        for d in range(1, Z):
            for k in (2 * kw, 2 * kw + 1):
                z_step(qg, 1, k, d)
            if helped:
                add(1, qg, pe, rows, d)
            if not helped or d < Z - 2:
                add(1, qg, pc, rows, d)
        if helped:
            we[rows, :] = acc_e[...].astype(BF)
            for k in (2 * kw, 2 * kw + 1):
                end_copy(k).start()
            add(1, qg, pc, rows, Z - 2)
            add(1, qg, pc, rows, Z - 1)
        out_ref[pl.ds(pl.multiple_of(l * lr + kw * cw, cw), cw), :] = acc[rows, :].astype(BF)
        w_sends(kw)

    if helped:
        @pl.when(middle)
        def _():
            for kw in range(nw):
                last_product(kw)

        @pl.when(jnp.logical_not(middle))
        def _():
            for k in range(nc):
                end_copy(k).wait_recv()
                for t in (via(k), 3 - via(k)):
                    turn_copy(k, t, l, t - 1).start()
                if 0 < k < nc - 1:
                    w_turn(k - 1)

        w_turn(nc - 2)
        w_turn(nc - 1)

        @pl.when(middle)
        def _():
            for k in range(nc):
                end_copy(k).wait_send()
            for t in (1, 2):
                share_copy(t, l).wait_send()
            for q in range(1, R):
                for t in range(L):
                    pass_copy(q, t, r, flip(t)).wait_send()

        @pl.when(jnp.logical_not(middle))
        def _():
            far_copy().wait_send()
    else:
        for kw in range(nw):
            last_product(kw)

    for k in range(nc):
        z_drain(pg, 0, k)
        z_drain(qg, 1, k)
    for j in range(1, R):
        row_copy(hg, hs, hr, j, r).wait_send()
        row_copy(pc, cs, cr_sem, j, r).wait_send()
    for k in range(nc):
        if helped:
            for t in (1, 2):
                turn_copy(k, t, l, t - 1).wait_send()
                if t != via(k):
                    turn_copy(k, t, flip(t), t - 1).wait_recv()
            turn_copy(k, 3 - via(k), flip(via(k)), 2).wait_send()
            turn_copy(k, via(k), flip(3), 2).wait_recv()
            continue
        for j in range(1, L):
            w_copy(k, j, l).wait_send()
            w_copy(k, j, lax.rem(l + L - j, L)).wait_recv()


def solution(mesh):
    L, R, Z = mesh.shape["layer"], mesh.shape["row"], mesh.shape["col"]
    nc = 4 if Z <= 4 else 2

    def local(density, hamiltonian, density_mask, hamilton_mask, filter_mask):
        tr, tc = density.shape
        lr = tr // L
        vmem = pl.BlockSpec(memory_space=pltpu.VMEM)
        hbm = pl.BlockSpec(memory_space=pltpu.HBM)
        dma = pltpu.SemaphoreType.DMA
        extra = [
            pltpu.VMEM((2 * lr // nc, tc), F32),
            pltpu.VMEM((R * tr // tc, tc, tc), BF),
            pltpu.VMEM((lr, tc), BF),
            dma((2,)),
            dma((2,)),
            dma((R - 1, L)),
            dma((R - 1, L)),
            dma((nc,)),
            dma((nc,)),
            dma((1,)),
            dma((1,)),
        ] if Z == 4 and L == 4 else []
        return pl.pallas_call(
            functools.partial(kernel, L, R, Z, nc),
            out_shape=jax.ShapeDtypeStruct((tr, tc), BF),
            in_specs=[hbm, hbm, vmem],
            out_specs=vmem,
            scratch_shapes=[
                pltpu.VMEM((tr, tc), BF),
                pltpu.VMEM((tr, tc), BF),
                pltpu.VMEM((3, tr // BS, tc), F32),
                pltpu.VMEM((lr, tc), F32),
                pltpu.VMEM((Z, lr, tc), BF),
                pltpu.VMEM((Z, lr, tc), BF),
                pltpu.VMEM((R * tr // tc, tc, tc), BF),
                pltpu.VMEM((R * tr // tc, tc, tc), BF),
                dma((3,)),
                dma((2, 2, nc, Z - 1)),
                dma((2, 2, nc, Z - 1)),
                dma((R - 1,)),
                dma((R - 1,)),
                dma((R - 1,)),
                dma((R - 1,)),
                dma((L - 1, nc)),
                dma((L - 1, nc)),
            ] + extra,
            compiler_params=pltpu.CompilerParams(
                collective_id=0, has_side_effects=True, vmem_limit_bytes=52 * 2**20),
            cost_estimate=pl.CostEstimate(
                flops=4 * lr * tc * tc * Z, bytes_accessed=6 * tr * tc, transcendentals=0),
        )(density, hamiltonian, jnp.stack([density_mask.T, hamilton_mask.T, filter_mask.T]))

    placed = (P("row", "col"),) * 5
    return jax.shard_map(
        local, mesh=mesh, in_specs=placed, out_specs=P("row", "col"), check_vma=False)
```

```python
import functools

import jax
import jax.numpy as jnp
from jax import lax
from jax.experimental import pallas as pl
from jax.experimental.pallas import tpu as pltpu
from jax.sharding import PartitionSpec as P

BS = 64
BF = jnp.bfloat16
F32 = jnp.float32


def kernel(L, R, Z, nc, p_hbm, h_hbm, m_in, out_ref,
           p_in, h_in, em, acc, pg, qg, hg, pc, in_sem, zs, zr, hs, hr, cs, cr_sem, ws, wr,
           acc_e=None, pe=None, we=None, gs=None, gr=None, fs=None, fr=None, es=None, er=None,
           xs=None, xr=None):
    l, r, c = lax.axis_index("layer"), lax.axis_index("row"), lax.axis_index("col")
    tr, tc = p_in.shape
    lr = tr // L
    ch = lr // nc
    G = tr // tc
    nb, lb = tr // BS, lr // BS
    lrow = pl.multiple_of(l * lr, lr)
    nw = nc // 2
    cw = lr // nw
    helped = acc_e is not None
    middle = (c > 0) & (c < Z - 1)
    end = jnp.where(c <= 1, 0, Z - 1)

    first = pltpu.make_async_copy(
        p_hbm.at[pl.ds(lrow, lr)], pg.at[c], in_sem.at[0])
    whole_p = pltpu.make_async_copy(p_hbm, p_in, in_sem.at[1])
    whole_h = pltpu.make_async_copy(h_hbm, h_in, in_sem.at[2])
    first.start()
    whole_h.start()
    whole_p.start()

    barrier = pltpu.get_barrier_semaphore()

    def greet(dev):
        pl.semaphore_signal(barrier, inc=1, device_id=dev)

    @pl.when(c > 0)
    def _():
        greet({"col": c - 1})

    @pl.when(c < Z - 1)
    def _():
        greet({"col": c + 1})

    for j in range(1, R):
        greet({"row": lax.rem(r + j, R)})
    for j in range(1, L):
        greet({"layer": lax.rem(l + j, L)})

    spread = (lax.broadcasted_iota(jnp.int32, (tc // BS, tc), 1) // BS
              == lax.broadcasted_iota(jnp.int32, (tc // BS, tc), 0))
    spread = spread.astype(F32).astype(BF)
    for i in range(3):
        em[i] = lax.dot_general(
            m_in[i].astype(F32).astype(BF), spread, (((0,), (0,)), ((), ())),
            preferred_element_type=F32)

    def z_copy(buf, ph, k, side, origin, hop):
        view = buf.at[origin, pl.ds(k * ch, ch)]
        to = c + 1 if side == 0 else c - 1
        return pltpu.make_async_remote_copy(
            view, view, zs.at[ph, side, k, hop], zr.at[ph, side, k, hop],
            device_id={"col": to})

    def z_origin(side, d):
        return c - d if side == 0 else c + d

    def z_sends(ph, side, d):
        last = 1 if helped and ph == 1 else 0
        there = c < Z - 1 - last if side == 0 else c > last
        if d == 0:
            return there
        return there & (c >= d if side == 0 else c + d < Z)

    def z_gets(ph, side, d):
        got = c >= d if side == 0 else c + d < Z
        return got & middle if helped and ph == 1 else got

    def z_send(buf, ph, k, d):
        for side in range(2):
            @pl.when(z_sends(ph, side, d))
            def _():
                z_copy(buf, ph, k, side, z_origin(side, d), d).start()

    def z_step(buf, ph, k, d):
        for side in range(2):
            @pl.when(z_gets(ph, side, d))
            def _():
                z_copy(buf, ph, k, side, z_origin(side, d), d - 1).wait_recv()
        if d < Z - 1:
            z_send(buf, ph, k, d)

    def z_drain(buf, ph, k):
        for d in range(Z - 1):
            for side in range(2):
                @pl.when(z_sends(ph, side, d))
                def _():
                    z_copy(buf, ph, k, side, z_origin(side, d), d).wait_send()

    def mask_chunk(k):
        for i in range(ch // BS):
            at = k * (ch // BS) + i
            keep = em[0, pl.ds(l * lb + at, 1), :].astype(BF)
            rows = pl.ds(at * BS, BS)
            pg[c, rows, :] = pg[c, rows, :] * keep

    first.wait()
    near = jnp.where(c > 0, 1, 0) + jnp.where(c < Z - 1, 1, 0)
    for k in range(nc):
        mask_chunk(k)
        if k == 0:
            pl.semaphore_wait(barrier, near + (R - 1) + (L - 1))
        if k < 2:
            z_send(pg, 0, k, 0)

    def fill(src, dst, e):
        per = tc // BS

        def body(i, carry):
            keep = em[e, pl.ds(i, 1), :].astype(BF)
            dst[r * G + i // per, pl.ds(pl.multiple_of((i % per) * BS, BS), BS), :] = (
                src[pl.ds(pl.multiple_of(i * BS, BS), BS), :] * keep)
            return carry

        lax.fori_loop(0, nb, body, 0)

    def row_copy(buf, ss, rs, j, owner):
        view = buf.at[pl.ds(owner * G, G)]
        return pltpu.make_async_remote_copy(
            view, view, ss.at[j - 1], rs.at[j - 1], device_id={"row": lax.rem(r + j, R)})

    whole_h.wait()
    fill(h_in, hg, 1)
    for j in range(1, R):
        row_copy(hg, hs, hr, j, r).start()
    whole_p.wait()
    fill(p_in, pc, 0)
    for j in range(1, R):
        row_copy(pc, cs, cr_sem, j, r).start()

    def begin(left, right, rows):
        acc[rows, :] = jnp.dot(left[c, rows, :], right[c], preferred_element_type=F32)

    def add(ph, left, right, rows, d):
        for side in range(2):
            @pl.when(z_gets(ph, side, d))
            def _():
                o = z_origin(side, d)
                if right is pe and helped:
                    acc_e[...] += jnp.dot(left[o, rows, :], pe[o], preferred_element_type=F32)
                else:
                    acc[rows, :] += jnp.dot(left[o, rows, :], right[o], preferred_element_type=F32)

    def share(row, layer):
        start = layer * lr
        return pe.at[row * G + start // tc, pl.ds(pl.multiple_of(start % tc, lr), lr)]

    def flip(t):
        return (l, l + 1 - 2 * (l % 2), l + 2 - 4 * (l // 2), L - 1 - l)[t]

    def share_copy(t, layer):
        return pltpu.make_async_remote_copy(
            share(r, layer), share(r, layer), gs.at[t - 1], gr.at[t - 1],
            device_id={"layer": flip(t)})

    beside = jnp.where(c == 1, 0, jnp.where(c == 0, 1, jnp.where(c == Z - 1, Z - 2, Z - 1)))

    def far_copy():
        start = flip(3) * lr
        view = pc.at[r * G + start // tc, pl.ds(pl.multiple_of(start % tc, lr), lr)]
        return pltpu.make_async_remote_copy(
            view, share(r, flip(3)), xs.at[0], xr.at[0], device_id={"col": beside})

    def pass_copy(q, i, row, layer):
        return pltpu.make_async_remote_copy(
            share(row, layer), share(row, layer), fs.at[q - 1, i], fr.at[q - 1, i],
            device_id={"row": lax.rem(r + q, R)})

    def end_copy(k):
        return pltpu.make_async_remote_copy(
            we.at[pl.ds(k * ch, ch)],
            out_ref.at[pl.ds(pl.multiple_of(l * lr + k * ch, ch), ch)],
            es.at[k], er.at[k], device_id={"col": beside})

    def w_copy(k, j, owner):
        view = out_ref.at[pl.ds(pl.multiple_of(owner * lr + k * ch, ch), ch)]
        return pltpu.make_async_remote_copy(
            view, view, ws.at[j - 1, k], wr.at[j - 1, k],
            device_id={"layer": lax.rem(l + j, L)})

    for kw in range(nw):
        pair = pl.ds(kw * cw, cw)
        for d in range(1, Z):
            for k in (2 * kw, 2 * kw + 1):
                z_step(pg, 0, k, d)
            if d == 1:
                for k in (2 * kw + 2, 2 * kw + 3):
                    if k < nc:
                        z_send(pg, 0, k, 0)
                if kw == 0:
                    for j in range(1, R):
                        row_copy(hg, hs, hr, j, lax.rem(r + R - j, R)).wait_recv()
                if kw == nw - 1 and helped:
                    @pl.when(jnp.logical_not(middle))
                    def _():
                        far_copy().start()

                    @pl.when(middle)
                    def _():
                        share(r, l)[...] = pg[end]
                        for t in (1, 2):
                            share_copy(t, l).start()
                        for q in range(1, R):
                            pass_copy(q, 0, r, l).start()
                begin(pg, hg, pair)
            add(0, pg, hg, pair, d)
        for k in (2 * kw, 2 * kw + 1):
            for i in range(ch // BS):
                at = k * (ch // BS) + i
                rows = pl.ds(at * BS, BS)
                keep = em[2, pl.ds(l * lb + at, 1), :].astype(BF)
                qg[c, rows, :] = acc[rows, :].astype(BF) * keep
            z_send(qg, 1, k, 0)

    for j in range(1, R):
        row_copy(pc, cs, cr_sem, j, lax.rem(r + R - j, R)).wait_recv()

    def turn_copy(k, t, owner, lane):
        view = out_ref.at[pl.ds(pl.multiple_of(owner * lr + k * ch, ch), ch)]
        return pltpu.make_async_remote_copy(
            view, view, ws.at[lane, k], wr.at[lane, k], device_id={"layer": flip(t)})

    def via(k):
        return 1 + k % 2

    def w_sends(kw):
        if not helped:
            for k in (2 * kw, 2 * kw + 1):
                for j in range(1, L):
                    w_copy(k, j, l).start()
            return
        for i in range(2):
            for t in (1, 2):
                turn_copy(2 * kw + (i + t + 1) % 2, t, l, t - 1).start()
        if kw > 0:
            w_turn(2 * kw - 2)
            w_turn(2 * kw - 1)

    def w_turn(k):
        t = via(k)
        turn_copy(k, t, flip(t), t - 1).wait_recv()
        turn_copy(k, 3 - t, flip(t), 2).start()

    def last_product(kw):
        rows = pl.ds(kw * cw, cw)
        begin(qg, pc, rows)
        if helped:
            if kw == 0:
                for t in (1, 2):
                    share_copy(t, flip(t)).wait_recv()
                    for q in range(1, R):
                        pass_copy(q, t, r, flip(t)).start()
                far_copy().wait_recv()
                for q in range(1, R):
                    pass_copy(q, 3, r, flip(3)).start()
                for q in range(1, R):
                    row = lax.rem(r + R - q, R)
                    for t in range(L):
                        pass_copy(q, t, row, flip(t)).wait_recv()
            acc_e[...] = jnp.dot(qg[c, rows, :], pe[c], preferred_element_type=F32)
        for d in range(1, Z):
            for k in (2 * kw, 2 * kw + 1):
                z_step(qg, 1, k, d)
            if helped:
                add(1, qg, pe, rows, d)
            if not helped or d < Z - 2:
                add(1, qg, pc, rows, d)
        if helped:
            we[rows, :] = acc_e[...].astype(BF)
            for k in (2 * kw, 2 * kw + 1):
                end_copy(k).start()
            add(1, qg, pc, rows, Z - 2)
            add(1, qg, pc, rows, Z - 1)
        out_ref[pl.ds(pl.multiple_of(l * lr + kw * cw, cw), cw), :] = acc[rows, :].astype(BF)
        w_sends(kw)

    if helped:
        @pl.when(middle)
        def _():
            for kw in range(nw):
                last_product(kw)

        @pl.when(jnp.logical_not(middle))
        def _():
            for k in range(nc):
                end_copy(k).wait_recv()
                for t in (via(k), 3 - via(k)):
                    turn_copy(k, t, l, t - 1).start()
                if 0 < k < nc - 1:
                    w_turn(k - 1)

        w_turn(nc - 2)
        w_turn(nc - 1)

        @pl.when(middle)
        def _():
            for k in range(nc):
                end_copy(k).wait_send()
            for t in (1, 2):
                share_copy(t, l).wait_send()
            for q in range(1, R):
                for t in range(L):
                    pass_copy(q, t, r, flip(t)).wait_send()

        @pl.when(jnp.logical_not(middle))
        def _():
            far_copy().wait_send()
    else:
        for kw in range(nw):
            last_product(kw)

    for k in range(nc):
        z_drain(pg, 0, k)
        z_drain(qg, 1, k)
    for j in range(1, R):
        row_copy(hg, hs, hr, j, r).wait_send()
        row_copy(pc, cs, cr_sem, j, r).wait_send()
    for k in range(nc):
        if helped:
            for t in (1, 2):
                turn_copy(k, t, l, t - 1).wait_send()
                if t != via(k):
                    turn_copy(k, t, flip(t), t - 1).wait_recv()
            turn_copy(k, 3 - via(k), flip(via(k)), 2).wait_send()
            turn_copy(k, via(k), flip(3), 2).wait_recv()
            continue
        for j in range(1, L):
            w_copy(k, j, l).wait_send()
            w_copy(k, j, lax.rem(l + L - j, L)).wait_recv()


def solution(mesh):
    L, R, Z = mesh.shape["layer"], mesh.shape["row"], mesh.shape["col"]
    nc = 4 if Z <= 4 else 2

    def local(density, hamiltonian, density_mask, hamilton_mask, filter_mask):
        tr, tc = density.shape
        lr = tr // L
        vmem = pl.BlockSpec(memory_space=pltpu.VMEM)
        hbm = pl.BlockSpec(memory_space=pltpu.HBM)
        dma = pltpu.SemaphoreType.DMA
        extra = [
            pltpu.VMEM((2 * lr // nc, tc), F32),
            pltpu.VMEM((R * tr // tc, tc, tc), BF),
            pltpu.VMEM((lr, tc), BF),
            dma((2,)),
            dma((2,)),
            dma((R - 1, L)),
            dma((R - 1, L)),
            dma((nc,)),
            dma((nc,)),
            dma((1,)),
            dma((1,)),
        ] if Z == 4 and L == 4 else []
        return pl.pallas_call(
            functools.partial(kernel, L, R, Z, nc),
            out_shape=jax.ShapeDtypeStruct((tr, tc), BF),
            in_specs=[hbm, hbm, vmem],
            out_specs=vmem,
            scratch_shapes=[
                pltpu.VMEM((tr, tc), BF),
                pltpu.VMEM((tr, tc), BF),
                pltpu.VMEM((3, tr // BS, tc), F32),
                pltpu.VMEM((lr, tc), F32),
                pltpu.VMEM((Z, lr, tc), BF),
                pltpu.VMEM((Z, lr, tc), BF),
                pltpu.VMEM((R * tr // tc, tc, tc), BF),
                pltpu.VMEM((R * tr // tc, tc, tc), BF),
                dma((3,)),
                dma((2, 2, nc, Z - 1)),
                dma((2, 2, nc, Z - 1)),
                dma((R - 1,)),
                dma((R - 1,)),
                dma((R - 1,)),
                dma((R - 1,)),
                dma((L - 1, nc)),
                dma((L - 1, nc)),
            ] + extra,
            compiler_params=pltpu.CompilerParams(
                collective_id=0, has_side_effects=True, vmem_limit_bytes=52 * 2**20),
            cost_estimate=pl.CostEstimate(
                flops=4 * lr * tc * tc * Z, bytes_accessed=6 * tr * tc, transcendentals=0),
        )(density, hamiltonian, jnp.stack([density_mask.T, hamilton_mask.T, filter_mask.T]))

    placed = (P("row", "col"),) * 5
    return jax.shard_map(
        local, mesh=mesh, in_specs=placed, out_specs=P("row", "col"), check_vma=False)
```
